128 devices in a mesh: chan: 64 (over z, x, y_lo, core), win: 2 (over y_hi).
Axes of the slice: x: 4, y: 4 (y_hi: 2, y_lo: 2; y = y_hi * 2 + y_lo), z: 4, core: 2. Of those that a mesh axis runs over, the one named last changes fastest.
Arguments:
- series: bfloat16 [32, 3000, 8192], P('win', None, 'chan'), may hold values from -96 to 96
- block_ids: int32 [4], replicated, may hold values from 0 to 63
Outputs:
- stacked: bfloat16 [96, 512, 2, 8192], P('win', None, None, 'chan')
The draws below stay inside these ranges and needn't reach their ends.
All inputs are finite; a program needn't handle non-finite values.
Results may differ from the reference program's by a relative error of at most 0.0056.
Values may be sent and summed in bfloat16 or wider, within the bound.
A program may use at most 192 MiB of HBM per device.

```python
import math
import jax
import jax.numpy as jnp
from jax import lax

SAMPLES = 3000
F_LO = 6
NFREQ = 96
BLOCK = 128
NSB = 4
CHANNELS = 8192
WINDOWS = 32


def draw_series(key, part):
    key = jax.random.fold_in(key, 7)
    keys = jax.random.split(key, 5)
    shape = (WINDOWS, SAMPLES, CHANNELS)
    small = (WINDOWS, 1, CHANNELS)
    positions = jnp.arange(SAMPLES, dtype=jnp.int32).reshape(1, SAMPLES, 1)
    noise = jnp.clip(jax.random.normal(keys[0], shape, jnp.float32), -4.0, 4.0)
    top = math.log(8.0)
    scale = jnp.exp(jax.random.uniform(keys[1], small, jnp.float32, 0.0, top))
    bins = jax.random.randint(keys[2], small, F_LO, F_LO + NFREQ)
    amplitude = jax.random.uniform(keys[3], small, jnp.float32, 0.5, 3.0)
    offset = jax.random.uniform(keys[4], small, jnp.float32, -math.pi, math.pi)
    angle = 2.0 * math.pi / SAMPLES * (bins * positions % SAMPLES).astype(jnp.float32) + offset
    values = scale * (noise + amplitude * jnp.sin(angle))
    return values.astype(jnp.bfloat16)


def touch_ends(values, rng, least, high):
    dims = values.shape
    index_at = [jax.random.randint(jax.random.fold_in(rng, axis), (), 0, dims[axis]) for axis in range(len(dims))]
    values = values.at[tuple(index_at)].set(least)
    longest = dims.index(max(dims))
    index_at[longest] = (index_at[longest] + 1) % dims[longest]
    return values.at[tuple(index_at)].set(high)


def setup_inputs(seed: int = 0) -> dict:
    seeds = jax.random.split(jax.random.key(seed), 3)
    series = draw_series(jax.random.fold_in(seeds[2], 71), 0)
    block_ids = touch_ends(jax.random.randint(seeds[1], (NSB,), 0, CHANNELS // BLOCK), jax.random.fold_in(seeds[1], 1), 0, (CHANNELS // BLOCK) - 1).astype(jnp.int32)
    return {"series": series, "block_ids": block_ids}


def make_tables():
    positions = jnp.arange(SAMPLES, dtype=jnp.int32)
    bins = F_LO + jnp.arange(NFREQ, dtype=jnp.int32)
    phases = bins[:, None] * positions[None, :] % SAMPLES
    angles = 2.0 * math.pi / SAMPLES * phases.astype(jnp.float32)
    table = jnp.concatenate([jnp.cos(angles), -jnp.sin(angles)], axis=0).astype(jnp.bfloat16)
    hann = 0.5 - 0.5 * jnp.cos(2.0 * math.pi / SAMPLES * positions.astype(jnp.float32))
    return (table, hann)

def reference(series, block_ids):
    table, hann = make_tables()

    def one_window(record):
        values = record.astype(jnp.float32)
        level = jnp.sqrt(lax.optimization_barrier(jnp.mean(values * values, axis=0, keepdims=True)) + 1e-06)
        clipped = jnp.clip(values, -2.0 * level, 2.0 * level)
        tapered = (clipped * hann[:, None]).astype(jnp.bfloat16)
        spectrum = jnp.dot(table, tapered, preferred_element_type=jnp.float32)
        power = lax.optimization_barrier(jnp.sum(spectrum * spectrum, axis=0, keepdims=True)) / NFREQ
        whitened = (spectrum * lax.rsqrt(power + 1e-06)).astype(jnp.bfloat16)
        return whitened.reshape(2, NFREQ, CHANNELS)
    whitened = lax.map(one_window, series)
    columns = (block_ids[:, None] * BLOCK + jnp.arange(BLOCK, dtype=jnp.int32)[None, :]).reshape(-1).astype(jnp.int32)
    sources = jnp.take(whitened, columns, axis=3)
    left = jnp.concatenate([sources[:, 0], sources[:, 1]], axis=0)
    right = jnp.stack([jnp.concatenate([whitened[:, 0], whitened[:, 1]], axis=0), jnp.concatenate([whitened[:, 1], -whitened[:, 0]], axis=0)], axis=2)
    left_f = jnp.transpose(left, (1, 0, 2))
    right_f = jnp.transpose(right, (1, 0, 2, 3))

    def one_freq(pair):
        lhs, rhs = pair
        total = jnp.einsum('ws,wpc->spc', lhs.astype(jnp.float32), rhs.astype(jnp.float32))
        return (total / WINDOWS).astype(jnp.bfloat16)
    return lax.map(one_freq, (left_f, right_f))
```

```python
import functools
import math

import jax
import jax.numpy as jnp
import numpy as np
from jax import lax
from jax.experimental import pallas as pl
from jax.experimental.pallas import tpu as pltpu
from jax.sharding import PartitionSpec as P

LENGTH = 3000
F_LO = 6
NFREQ = 96
WINDOWS = 32
HALF = NFREQ // 2
WINS = WINDOWS // 2
UNITS = 2 * HALF
MESH = pl.DeviceIdType.MESH
COL = (((0,), (0,)), ((), ()))


def make_table():
    positions = np.arange(LENGTH)
    bins = F_LO + np.arange(NFREQ)
    angles = 2.0 * math.pi / LENGTH * (bins[:, None] * positions[None, :] % LENGTH)
    hann = 0.5 - 0.5 * np.cos(2.0 * math.pi / LENGTH * positions)
    rows = np.stack([np.cos(angles), -np.sin(angles)], axis=1).reshape(2 * NFREQ, LENGTH)
    return jnp.asarray(rows * hann[None, :], jnp.bfloat16)


def spectra_kernel(table_ref, series_ref, out_ref, rows_ref):
    step = pl.program_id(0)
    clipped = []
    for k in range(2):
        values = series_ref[k].astype(jnp.float32)
        level = 2.0 * jnp.sqrt(jnp.mean(values * values, axis=0, keepdims=True) + 1e-6)
        clipped.append(jnp.clip(values, -level, level).astype(jnp.bfloat16))
    spectrum = jnp.dot(
        table_ref[...], jnp.concatenate(clipped, axis=1), preferred_element_type=jnp.float32
    )
    power = jnp.sum(spectrum * spectrum, axis=0, keepdims=True) / NFREQ
    whitened = spectrum * lax.rsqrt(power + 1e-6)
    for k in range(2):
        rows_ref[pl.ds(2 * step + k, 2 * NFREQ, WINS), :] = whitened[:, 128 * k : 128 * (k + 1)]

    @pl.when(step == WINS // 2 - 1)
    def _():
        out_ref[...] = rows_ref[...].reshape(2 * NFREQ, WINS, 128).astype(jnp.bfloat16)


def spectra(series):
    return pl.pallas_call(
        spectra_kernel,
        grid=(WINS // 2,),
        in_specs=[
            pl.BlockSpec((2 * NFREQ, LENGTH), lambda i: (0, 0)),
            pl.BlockSpec((2, LENGTH, 128), lambda i: (i, 0, 0)),
        ],
        out_specs=pl.BlockSpec((2 * NFREQ, WINS, 128), lambda i: (0, 0, 0)),
        out_shape=jax.ShapeDtypeStruct((2 * NFREQ, WINS, 128), jnp.bfloat16),
        scratch_shapes=[pltpu.VMEM((2 * NFREQ * WINS, 128), jnp.float32)],
        compiler_params=pltpu.CompilerParams(vmem_limit_bytes=58 * 2**20),
    )(make_table(), series)


def exchange_kernel(
    ids_ref, v_ref, src_ref, rhs_ref, p1, q1, p2, q2, p3, q3,
    win_sem, a1_send, a1_recv, a2_send, a2_recv, y_send, y_recv,
    b1_send, b1_recv, b2_send, b2_recv, c_send, c_recv, l_sem,
):
    me = lax.axis_index("chan")
    w = lax.axis_index("win")
    z, x, y, c = me // 16, me // 4 % 4, me // 2 % 2, me % 2

    def chan(z, x, y, c):
        return ((z * 4 + x) * 2 + y) * 2 + c

    def plane(h, a, b, c):
        return chan(jnp.where(h == 0, a, b), jnp.where(h == 0, b, a), y, c)

    ring = [(k, m) for k in range(4) for m in range(2) if (k, m) != (0, 0)]
    column = [(1, 0), (0, 1), (1, 1)]
    coords = (z, x)

    barrier = pltpu.get_barrier_semaphore()
    peers = [(plane(0, (z + k) % 4, x, (c + m) % 2), w) for k, m in ring]
    peers += [(plane(1, (x + k) % 4, z, (c + m) % 2), w) for k, m in ring if k]
    peers += [(chan(z, x, (y + dy) % 2, c), (w + dw) % 2) for dy, dw in column]
    for peer in peers:
        pl.semaphore_signal(barrier, inc=1, device_id=peer, device_id_type=MESH)
    pl.semaphore_wait(barrier, len(peers))

    def remote(src, dst, send, recv, peer):
        copy = pltpu.make_async_remote_copy(
            src_ref=src, dst_ref=dst, send_sem=send, recv_sem=recv,
            device_id=peer, device_id_type=MESH,
        )
        copy.start()
        return copy

    first = []
    for k, m in ring:
        for h in range(2):
            a, b = coords[h], coords[1 - h]
            to_a, to_c = (a + k) % 4, (c + m) % 2
            slot = k * 2 + m
            first.append(
                remote(
                    v_ref.at[pl.ds(h * UNITS + (to_a * 2 + to_c) * 12, 12)],
                    p1.at[h, a * 2 + c],
                    a1_send.at[h, slot], a1_recv.at[h, slot],
                    (plane(h, to_a, b, to_c), w),
                )
            )
    window = remote(
        v_ref.at[pl.ds((1 - w) * UNITS, UNITS)], rhs_ref.at[w],
        win_sem.at[0], win_sem.at[1], (me, 1 - w),
    )
    own_rhs = pltpu.make_async_copy(v_ref.at[pl.ds(w * UNITS, UNITS)], rhs_ref.at[w], l_sem.at[0])
    own_rhs.start()
    for h in range(2):
        a = coords[h]
        p1[h, a * 2 + c] = v_ref[pl.ds(h * UNITS + (a * 2 + c) * 12, 12)]
    for copy in first:
        copy.wait()

    where = []
    for j in range(4):
        block = ids_ref[j]
        where.append((block // 16, block // 4 % 4, block // 2 % 2, block % 2))

    second = []
    for h in range(2):
        a, b = coords[h], coords[1 - h]
        for j in range(4):
            own = where[j]
            q1[h, j] = p1[h, own[h] * 2 + own[3]]
        for k in range(1, 4):
            to_b = (b + k) % 4
            second.append(
                remote(
                    q1.at[h, :, pl.ds(to_b * 3, 3)], p2.at[h, b],
                    a2_send.at[h, k], a2_recv.at[h, k],
                    (plane(h, a, to_b, c), w),
                )
            )
        p2[h, b] = q1[h, :, pl.ds(b * 3, 3)]
    for copy in second:
        copy.wait()

    third = []
    for h in range(2):
        for j in range(4):
            q2[h, j] = p2[h, where[j][1 - h], j]
    for n, (dy, dw) in enumerate(column):
        to_y, to_w = (y + dy) % 2, (w + dw) % 2
        third.append(
            remote(
                q2.at[to_w], p3.at[w, y], y_send.at[n], y_recv.at[n],
                (chan(z, x, to_y, c), to_w),
            )
        )
    p3[w, y] = q2[w]
    for copy in third:
        copy.wait()
    for j in range(4):
        for g in range(2):
            q3[j, g] = p3[g, where[j][2], j]

    a = jnp.where(w == 0, z, x)
    b = jnp.where(w == 0, x, z)
    keep = pltpu.make_async_copy(q3, src_ref.at[:, :, a, c, b], l_sem.at[1])
    keep.start()
    pairs = (pl.ds(0, 2), pl.ds(2, 2))
    fourth = []
    for k in range(1, 4):
        for g in range(2):
            to = ((a + k) % 4, b) if g == 0 else (a, (b + k) % 4)
            fourth.append(
                remote(
                    q3.at[pairs[g]], src_ref.at[pairs[g], :, a, c, b],
                    b1_send.at[g, k], b1_recv.at[g, k],
                    (plane(w, to[0], to[1], c), w),
                )
            )
    keep.wait()
    for copy in fourth:
        copy.wait()

    def line(g, a, b):
        if g == 0:
            return src_ref.at[pairs[0], :, :, c, b]
        return src_ref.at[pairs[1], :, a, c, :]

    fifth = []
    for k in range(1, 4):
        for g in range(2):
            to = (a, (b + k) % 4) if g == 0 else ((a + k) % 4, b)
            fifth.append(
                remote(
                    line(g, a, b), line(g, a, b), b2_send.at[g, k], b2_recv.at[g, k],
                    (plane(w, to[0], to[1], c), w),
                )
            )
    sibling = (chan(z, x, y, 1 - c), w)
    last = []
    for g in range(2):
        last.append(
            remote(line(g, a, b), line(g, a, b), c_send.at[g, 0], c_recv.at[g, 0], sibling)
        )
    number = 0
    for k in range(1, 4):
        for g in range(2):
            fifth[number].wait()
            number += 1
            ref = line(g, (a - k + 4) % 4, (b - k + 4) % 4)
            last.append(remote(ref, ref, c_send.at[g, k], c_recv.at[g, k], sibling))
    for copy in last:
        copy.wait()
    window.wait()
    own_rhs.wait()


def exchange(block_ids, white):
    dma = pltpu.SemaphoreType.DMA
    vmem = lambda *shape: pltpu.VMEM(shape + (WINS, 128), jnp.bfloat16)
    return pl.pallas_call(
        exchange_kernel,
        out_shape=[
            jax.ShapeDtypeStruct((4, 2, 4, 2, 4, 3, WINS, 128), jnp.bfloat16),
            jax.ShapeDtypeStruct((2, UNITS, WINS, 128), jnp.bfloat16),
        ],
        in_specs=[
            pl.BlockSpec(memory_space=pltpu.SMEM),
            pl.BlockSpec(memory_space=pltpu.VMEM),
        ],
        out_specs=[pl.BlockSpec(memory_space=pl.ANY), pl.BlockSpec(memory_space=pl.ANY)],
        scratch_shapes=[
            vmem(2, 8, 12), vmem(2, 4, 12), vmem(2, 4, 4, 3), vmem(2, 4, 3),
            vmem(2, 2, 4, 3), vmem(4, 2, 3),
            dma((2,)), dma((2, 8)), dma((2, 8)), dma((2, 4)), dma((2, 4)), dma((3,)), dma((3,)),
            dma((2, 4)), dma((2, 4)), dma((2, 4)), dma((2, 4)), dma((2, 4)), dma((2, 4)), dma((2,)),
        ],
        compiler_params=pltpu.CompilerParams(
            collective_id=0, has_side_effects=True, vmem_limit_bytes=40 * 2**20
        ),
    )(block_ids, white)


def stack_kernel(count, src_ref, rhs_ref, out_ref, rows_ref):
    for i in range(count):
        left = jnp.concatenate(
            [src_ref[j, :, 2 * i : 2 * i + 2].reshape(4 * WINS, 128) for j in range(4)], axis=1
        )
        real = [rhs_ref[g, 2 * i] * (1.0 / WINDOWS) for g in range(2)]
        imag = [rhs_ref[g, 2 * i + 1] * (1.0 / WINDOWS) for g in range(2)]
        right = jnp.concatenate(
            [
                jnp.concatenate([real[0], imag[0], real[1], imag[1]], axis=0),
                jnp.concatenate([imag[0], -real[0], imag[1], -real[1]], axis=0),
            ],
            axis=1,
        )
        total = lax.dot_general(left, right, COL, preferred_element_type=jnp.float32)
        rows_ref[i % 2, pl.ds(0, 512, 2), :] = total[:, :128]
        rows_ref[i % 2, pl.ds(1, 512, 2), :] = total[:, 128:]
        out_ref[i] = rows_ref[i % 2].astype(jnp.bfloat16)


def stack(sources, rhs):
    count = 8
    out = pl.pallas_call(
        functools.partial(stack_kernel, count),
        grid=(HALF // count,),
        in_specs=[
            pl.BlockSpec((4, 2, 2 * count, WINS, 128), lambda i: (0, 0, i, 0, 0)),
            pl.BlockSpec((2, 2 * count, WINS, 128), lambda i: (0, i, 0, 0)),
        ],
        out_specs=pl.BlockSpec((count, 1024, 128), lambda i: (i, 0, 0)),
        out_shape=jax.ShapeDtypeStruct((HALF, 1024, 128), jnp.bfloat16),
        scratch_shapes=[pltpu.VMEM((2, 1024, 128), jnp.float32)],
        compiler_params=pltpu.CompilerParams(vmem_limit_bytes=40 * 2**20),
    )(sources.reshape(4, 2, UNITS, WINS, 128), rhs)
    return out.reshape(HALF, 512, 2, 128)


def local(series, block_ids):
    sources, rhs = exchange(block_ids, spectra(series))
    return stack(sources, rhs)


def solution(mesh):
    return jax.shard_map(
        local,
        mesh=mesh,
        in_specs=(P("win", None, "chan"), P()),
        out_specs=P("win", None, None, "chan"),
        check_vma=False,
    )
```

```python
import functools
import math

import jax
import jax.numpy as jnp
import numpy as np
from jax import lax
from jax.experimental import pallas as pl
from jax.experimental.pallas import tpu as pltpu
from jax.sharding import PartitionSpec as P

LENGTH = 3000
F_LO = 6
NFREQ = 96
WINDOWS = 32
HALF = NFREQ // 2
WINS = WINDOWS // 2
PART = WINS // 2
GROUP = 4
MESH = pl.DeviceIdType.MESH
COL = (((0,), (0,)), ((), ()))


def make_table():
    positions = np.arange(LENGTH)
    bins = F_LO + np.arange(NFREQ)
    angles = 2.0 * math.pi / LENGTH * (bins[:, None] * positions[None, :] % LENGTH)
    hann = 0.5 - 0.5 * np.cos(2.0 * math.pi / LENGTH * positions)
    rows = np.stack([np.cos(angles), -np.sin(angles)], axis=1).reshape(2 * NFREQ, LENGTH)
    return jnp.asarray(rows * hann[None, :], jnp.bfloat16)


def exchange_kernel(
    ids_ref, table_ref, series_ref, src_ref, rhs_ref,
    held, rows, v, p1_0, p1_1, q1, p2_0, p2_1, q2, p3, q3,
    s_sem, l_sem, w_send, w_recv, a1_send, a1_recv, a2_send, a2_recv, y_send, y_recv,
    b1_send, b1_recv, b2_send, b2_recv, c_send, c_recv,
):
    me = lax.axis_index("chan")
    w = lax.axis_index("win")
    z, x, y, c = me // 16, me // 4 % 4, me // 2 % 2, me % 2

    def chan(z, x, y, c):
        return ((z * 4 + x) * 2 + y) * 2 + c

    def plane(h, a, b, c):
        return chan(jnp.where(h == 0, a, b), jnp.where(h == 0, b, a), y, c)

    p1 = (p1_0, p1_1)
    p2 = (p2_0, p2_1)
    column = [(1, 0), (0, 1), (1, 1)]
    coords = (z, x)
    loads = []
    for n in range(WINS // GROUP):
        window = pl.ds(n * GROUP, GROUP)
        loads.append(pltpu.make_async_copy(series_ref.at[window], held.at[window], s_sem.at[n]))
        loads[-1].start()

    barrier = pltpu.get_barrier_semaphore()
    peers = [(plane(h, (coords[h] + k) % 4, coords[1 - h], (c + m) % 2), w)
             for h in range(2) for k in range(1, 4) for m in range(2)]
    peers += [(chan(z, x, y, 1 - c), w)]
    peers += [(chan(z, x, (y + dy) % 2, c), (w + dw) % 2) for dy, dw in column]
    for peer in peers:
        pl.semaphore_signal(barrier, inc=1, device_id=peer, device_id_type=MESH)

    def remote(src, dst, send, recv, peer):
        return pltpu.make_async_remote_copy(
            src_ref=src, dst_ref=dst, send_sem=send, recv_sem=recv,
            device_id=peer, device_id_type=MESH,
        )

    def transform(part, n):
        first = part * PART + n * GROUP
        clipped = []
        for k in range(GROUP):
            values = held[first + k].astype(jnp.float32)
            level = 2.0 * jnp.sqrt(jnp.mean(values * values, axis=0, keepdims=True) + 1e-6)
            clipped.append(jnp.clip(values, -level, level).astype(jnp.bfloat16))
        spectrum = jnp.dot(
            table_ref[...], jnp.concatenate(clipped, axis=1), preferred_element_type=jnp.float32
        )
        power = jnp.sum(spectrum * spectrum, axis=0, keepdims=True) / NFREQ
        whitened = spectrum * lax.rsqrt(power + 1e-6)
        for k in range(GROUP):
            rows[pl.ds(n * GROUP + k, 2 * NFREQ, PART), :] = whitened[:, 128 * k : 128 * (k + 1)]

    first = []
    windows = []
    for part in range(2):
        for n in range(PART // GROUP):
            loads[part * (PART // GROUP) + n].wait()
            transform(part, n)
        v[part] = rows[...].reshape(NFREQ, 2 * PART, 128).astype(jnp.bfloat16)
        if part == 0:
            pl.semaphore_wait(barrier, len(peers))
        other = (c + part) % 2
        for k in (1, 3, 2, 0):
            for h in range(2):
                a, b = coords[h], coords[1 - h]
                to_a = (a + k) % 4
                copy = remote(
                    v.at[part, pl.ds(h * HALF + to_a * 12, 12)], p1[h].at[a, c],
                    a1_send.at[part, h, k], a1_recv.at[h, k, other],
                    (plane(h, to_a, b, part if k else 1 - c), w),
                )
                if k:
                    copy.start()
                    first.append(copy)
                else:
                    pl.when(other == 1)(copy.start)
        windows.append(
            remote(
                v.at[part, pl.ds((1 - w) * HALF, HALF)], rhs_ref.at[w, part],
                w_send.at[part], w_recv.at[part], (me, 1 - w),
            )
        )
        windows[-1].start()
    own_rhs = pltpu.make_async_copy(v.at[:, pl.ds(w * HALF, HALF)], rhs_ref.at[w], l_sem.at[0])
    own_rhs.start()

    where = []
    for j in range(4):
        block = ids_ref[j]
        where.append((block // 16, block // 4 % 4, block // 2 % 2, block % 2))

    second = []
    for h in range(2):
        a, b = coords[h], coords[1 - h]
        p1[h][a, c] = v[c, pl.ds(h * HALF + a * 12, 12)]
        for k in range(4):
            for m in range(2):
                if k or m:
                    remote(
                        v.at[0, pl.ds(0, 12)], p1[h].at[a, c],
                        a1_send.at[0, h, k], a1_recv.at[h, k, m], (me, 1 - w),
                    ).wait_recv()
        for j in range(4):
            q1[h, j] = p1[h][where[j][h], where[j][3]]
        for k in (1, 3, 2):
            to_b = (b + k) % 4
            copy = remote(
                q1.at[h, :, pl.ds(to_b * 3, 3)], p2[h].at[b],
                a2_send.at[h, k], a2_recv.at[h, k], (plane(h, a, to_b, c), w),
            )
            copy.start()
            second.append(copy)
        p2[h][b] = q1[h, :, pl.ds(b * 3, 3)]

    for h in range(2):
        for copy in second[3 * h : 3 * h + 3]:
            copy.wait()
        for j in range(4):
            q2[h, j] = p2[h][where[j][1 - h], j]
    third = []
    for n, (dy, dw) in enumerate(column):
        to_y, to_w = (y + dy) % 2, (w + dw) % 2
        third.append(
            remote(
                q2.at[to_w], p3.at[w, y], y_send.at[n], y_recv.at[n],
                (chan(z, x, to_y, c), to_w),
            )
        )
        third[-1].start()
    p3[w, y] = q2[w]
    for copy in third:
        copy.wait()
    for j in range(4):
        for g in range(2):
            q3[j, g] = p3[g, where[j][2], j]

    a = jnp.where(w == 0, z, x)
    b = jnp.where(w == 0, x, z)
    slots = (pl.ds(0, 2), pl.ds(2, 2))

    def at(s, k, m):
        k, m = (4 - k) % 4, (4 - m) % 4
        return ((a + k) % 4, (b + m) % 4) if s == 0 else ((a + m) % 4, (b + k) % 4)

    def piece(s, k, m):
        pa, pb = at(s, k, m)
        return src_ref.at[slots[s], :, c, pa, pb]

    def line(s, m):
        pa, pb = at(s, 0, m)
        if s == 0:
            return src_ref.at[slots[s], :, c, :, pb]
        return src_ref.at[slots[s], :, c, pa]

    keep = pltpu.make_async_copy(q3, src_ref.at[:, :, c, a, b], l_sem.at[1])
    keep.start()
    fourth, fifth, last = {}, {}, []
    for k in (1, 3, 2):
        for s in range(2):
            to = at(s, 4 - k, 0)
            fourth[s, k] = remote(
                q3.at[slots[s]], piece(s, 0, 0), b1_send.at[s, k], b1_recv.at[s, k],
                (plane(w, to[0], to[1], c), w),
            )
            fourth[s, k].start()

    def forward(s, k):
        for m in (1, 3, 2):
            to = at(s, 0, 4 - m)
            fifth[s, k, m] = remote(
                q3.at[slots[s]] if k == 0 else piece(s, k, 0), piece(s, k, 0),
                b2_send.at[s, k, m], b2_recv.at[s, k, m], (plane(w, to[0], to[1], c), w),
            )
            fifth[s, k, m].start()

    for s in range(2):
        forward(s, 0)
    keep.wait()
    for k in (1, 3, 2):
        for s in range(2):
            fourth[s, k].wait()
            forward(s, k)
    sibling = (chan(z, x, y, 1 - c), w)
    for m in (0, 1, 3, 2):
        for s in range(2):
            if m:
                for k in range(4):
                    fifth[s, k, m].wait()
            last.append(remote(line(s, m), line(s, m), c_send.at[s, m], c_recv.at[s, m], sibling))
            last[-1].start()
    for copy in last:
        copy.wait()
    for copy in windows:
        copy.wait()
    own_rhs.wait()
    for copy in first:
        copy.wait_send()
    for h in range(2):
        remote(
            v.at[0, pl.ds(0, 12)], p1[h].at[0, 0], a1_send.at[1 - c, h, 0], a1_recv.at[h, 0, 1],
            sibling,
        ).wait_send()


def exchange(block_ids, series):
    dma = pltpu.SemaphoreType.DMA
    vmem = lambda *shape: pltpu.VMEM(shape + (2 * PART, 128), jnp.bfloat16)
    return pl.pallas_call(
        exchange_kernel,
        out_shape=[
            jax.ShapeDtypeStruct((4, 2, 2, 4, 4, 3, 2 * PART, 128), jnp.bfloat16),
            jax.ShapeDtypeStruct((2, 2, HALF, 2 * PART, 128), jnp.bfloat16),
        ],
        in_specs=[
            pl.BlockSpec(memory_space=pltpu.SMEM),
            pl.BlockSpec(memory_space=pltpu.VMEM),
            pl.BlockSpec(memory_space=pl.ANY),
        ],
        out_specs=[pl.BlockSpec(memory_space=pl.ANY), pl.BlockSpec(memory_space=pl.ANY)],
        scratch_shapes=[
            pltpu.VMEM((WINS, LENGTH, 128), jnp.bfloat16),
            pltpu.VMEM((2 * NFREQ * PART, 128), jnp.float32),
            vmem(2, NFREQ), vmem(4, 2, 12), vmem(4, 2, 12), vmem(2, 4, 12), vmem(4, 4, 3), vmem(4, 4, 3),
            vmem(2, 4, 3),
            vmem(2, 2, 4, 3), vmem(4, 2, 3),
            dma((WINS // GROUP,)), dma((2,)), dma((2,)), dma((2,)),
            dma((2, 2, 4)), dma((2, 4, 2)), dma((2, 4)), dma((2, 4)), dma((3,)), dma((3,)),
            dma((2, 4)), dma((2, 4)), dma((2, 4, 4)), dma((2, 4, 4)), dma((2, 4)), dma((2, 4)),
        ],
        compiler_params=pltpu.CompilerParams(
            collective_id=0, has_side_effects=True, vmem_limit_bytes=46 * 2**20
        ),
    )(block_ids, make_table(), series)


def stack_kernel(count, src_ref, rhs_ref, out_ref, rows_ref):
    for i in range(count):
        left = jnp.concatenate(
            [src_ref[j, :, :, i].reshape(8 * PART, 128) for j in range(4)], axis=1
        )
        tiles = [rhs_ref[g, part, i].astype(jnp.float32) * (1.0 / WINDOWS)
                 for g in range(2) for part in range(2)]
        turned = [t for tile in tiles for t in (tile[PART:], -tile[:PART])]
        right = jnp.concatenate(
            [jnp.concatenate(tiles, axis=0), jnp.concatenate(turned, axis=0)], axis=1
        ).astype(jnp.bfloat16)
        total = lax.dot_general(left, right, COL, preferred_element_type=jnp.float32)
        rows_ref[i % 2, pl.ds(0, 512, 2), :] = total[:, :128]
        rows_ref[i % 2, pl.ds(1, 512, 2), :] = total[:, 128:]
        out_ref[i] = rows_ref[i % 2].astype(jnp.bfloat16)


def stack(sources, rhs):
    count = 8
    out = pl.pallas_call(
        functools.partial(stack_kernel, count),
        grid=(HALF // count,),
        in_specs=[
            pl.BlockSpec((4, 2, 2, count, 2 * PART, 128), lambda i: (0, 0, 0, i, 0, 0)),
            pl.BlockSpec((2, 2, count, 2 * PART, 128), lambda i: (0, 0, i, 0, 0)),
        ],
        out_specs=pl.BlockSpec((count, 1024, 128), lambda i: (i, 0, 0)),
        out_shape=jax.ShapeDtypeStruct((HALF, 1024, 128), jnp.bfloat16),
        scratch_shapes=[pltpu.VMEM((2, 1024, 128), jnp.float32)],
        compiler_params=pltpu.CompilerParams(vmem_limit_bytes=40 * 2**20),
    )(sources.reshape(4, 2, 2, HALF, 2 * PART, 128), rhs)
    return out.reshape(HALF, 512, 2, 128)


def local(series, block_ids):
    sources, rhs = exchange(block_ids, series)
    return stack(sources, rhs)


def solution(mesh):
    return jax.shard_map(
        local,
        mesh=mesh,
        in_specs=(P("win", None, "chan"), P()),
        out_specs=P("win", None, None, "chan"),
        check_vma=False,
    )
```

```python
import functools
import math

import jax
import jax.numpy as jnp
import numpy as np
from jax import lax
from jax.experimental import pallas as pl
from jax.experimental.pallas import tpu as pltpu
from jax.sharding import PartitionSpec as P

LENGTH = 3000
F_LO = 6
NFREQ = 96
WINDOWS = 32
HALF = NFREQ // 2
WINS = WINDOWS // 2
PART = WINS // 2
GROUP = 4
MESH = pl.DeviceIdType.MESH
COL = (((0,), (0,)), ((), ()))


def make_table():
    positions = np.arange(LENGTH)
    bins = F_LO + np.arange(NFREQ)
    angles = 2.0 * math.pi / LENGTH * (bins[:, None] * positions[None, :] % LENGTH)
    hann = 0.5 - 0.5 * np.cos(2.0 * math.pi / LENGTH * positions)
    rows = np.stack([np.cos(angles), -np.sin(angles)], axis=1).reshape(2 * NFREQ, LENGTH)
    return jnp.asarray(rows * hann[None, :], jnp.bfloat16)


def product(left, right, pair):
    tiles = [tile.astype(jnp.float32) * (1.0 / WINDOWS) for tile in right]
    turned = [t for tile in tiles for t in (tile[PART:], -tile[:PART])]
    factor = jnp.concatenate(
        [jnp.concatenate(tiles, axis=0), jnp.concatenate(turned, axis=0)], axis=1
    ).astype(jnp.bfloat16)
    total = lax.dot_general(
        jnp.concatenate(left, axis=1), factor, COL, preferred_element_type=jnp.float32
    )
    pair[pl.ds(0, 256, 2), :] = total[:, :128]
    pair[pl.ds(1, 256, 2), :] = total[:, 128:]
    return pair[...].astype(jnp.bfloat16)


def exchange_kernel(
    ids_ref, table_ref, series_ref, done_ref, late_ref, rhs_out,
    held, rows, v, rhs_ref, src_ref, lines, pairs, p1_0, p1_1, q1, p2_0, p2_1, q2, p3, q3,
    s_sem, o_sem, l_sem, w_send, w_recv, a1_send, a1_recv, a2_send, a2_recv, y_send, y_recv,
    b1_send, b1_recv, b2_send, b2_recv, h_send, h_recv, c_send, c_recv,
):
    me = lax.axis_index("chan")
    w = lax.axis_index("win")
    z, x, y, c = me // 16, me // 4 % 4, me // 2 % 2, me % 2

    def chan(z, x, y, c):
        return ((z * 4 + x) * 2 + y) * 2 + c

    def plane(h, a, b, c):
        return chan(jnp.where(h == 0, a, b), jnp.where(h == 0, b, a), y, c)

    p1 = (p1_0, p1_1)
    p2 = (p2_0, p2_1)
    column = [(1, 0), (0, 1), (1, 1)]
    coords = (z, x)
    loads = []
    for n in range(WINS // GROUP):
        window = pl.ds(n * GROUP, GROUP)
        loads.append(pltpu.make_async_copy(series_ref.at[window], held.at[window], s_sem.at[n]))
        loads[-1].start()

    barrier = pltpu.get_barrier_semaphore()
    peers = [(plane(h, (coords[h] + k) % 4, coords[1 - h], (c + m) % 2), w)
             for h in range(2) for k in range(1, 4) for m in range(2)]
    peers += [(chan(z, x, y, 1 - c), w)]
    peers += [(chan(z, x, (y + dy) % 2, c), (w + dw) % 2) for dy, dw in column]
    for peer in peers:
        pl.semaphore_signal(barrier, inc=1, device_id=peer, device_id_type=MESH)

    def remote(src, dst, send, recv, peer):
        return pltpu.make_async_remote_copy(
            src_ref=src, dst_ref=dst, send_sem=send, recv_sem=recv,
            device_id=peer, device_id_type=MESH,
        )

    def transform(part, n):
        first = part * PART + n * GROUP
        clipped = []
        for k in range(GROUP):
            values = held[first + k].astype(jnp.float32)
            level = 2.0 * jnp.sqrt(jnp.mean(values * values, axis=0, keepdims=True) + 1e-6)
            clipped.append(jnp.clip(values, -level, level).astype(jnp.bfloat16))
        spectrum = jnp.dot(
            table_ref[...], jnp.concatenate(clipped, axis=1), preferred_element_type=jnp.float32
        )
        power = jnp.sum(spectrum * spectrum, axis=0, keepdims=True) / NFREQ
        whitened = spectrum * lax.rsqrt(power + 1e-6)
        for k in range(GROUP):
            rows[pl.ds(n * GROUP + k, 2 * NFREQ, PART), :] = whitened[:, 128 * k : 128 * (k + 1)]

    first = []
    windows = []
    for part in range(2):
        for n in range(PART // GROUP):
            loads[part * (PART // GROUP) + n].wait()
            transform(part, n)
        v[part] = rows[...].reshape(NFREQ, 2 * PART, 128).astype(jnp.bfloat16)
        if part == 0:
            pl.semaphore_wait(barrier, len(peers))
        other = (c + part) % 2
        for k in (1, 3, 2, 0):
            for h in range(2):
                a, b = coords[h], coords[1 - h]
                to_a = (a + k) % 4
                copy = remote(
                    v.at[part, pl.ds(h * HALF + to_a * 12, 12)], p1[h].at[a, c],
                    a1_send.at[part, h, k], a1_recv.at[h, k, other],
                    (plane(h, to_a, b, part if k else 1 - c), w),
                )
                if k:
                    copy.start()
                    first.append(copy)
                else:
                    pl.when(other == 1)(copy.start)
        windows.append(
            remote(
                v.at[part, pl.ds((1 - w) * HALF, HALF)], rhs_ref.at[w, part],
                w_send.at[part], w_recv.at[part], (me, 1 - w),
            )
        )
        windows[-1].start()
    own_rhs = pltpu.make_async_copy(v.at[:, pl.ds(w * HALF, HALF)], rhs_ref.at[w], l_sem.at[0])
    own_rhs.start()

    where = []
    for j in range(4):
        block = ids_ref[j]
        where.append((block // 16, block // 4 % 4, block // 2 % 2, block % 2))

    second = []
    for h in range(2):
        a, b = coords[h], coords[1 - h]
        p1[h][a, c] = v[c, pl.ds(h * HALF + a * 12, 12)]
        for k in range(4):
            for m in range(2):
                if k or m:
                    remote(
                        v.at[0, pl.ds(0, 12)], p1[h].at[a, c],
                        a1_send.at[0, h, k], a1_recv.at[h, k, m], (me, 1 - w),
                    ).wait_recv()
        for j in range(4):
            q1[h, j] = p1[h][where[j][h], where[j][3]]
        for k in (1, 3, 2):
            to_b = (b + k) % 4
            copy = remote(
                q1.at[h, :, pl.ds(to_b * 3, 3)], p2[h].at[b],
                a2_send.at[h, k], a2_recv.at[h, k], (plane(h, a, to_b, c), w),
            )
            copy.start()
            second.append(copy)
        p2[h][b] = q1[h, :, pl.ds(b * 3, 3)]

    for h in range(2):
        for copy in second[3 * h : 3 * h + 3]:
            copy.wait()
        for j in range(4):
            q2[h, j] = p2[h][where[j][1 - h], j]
    third = []
    for n, (dy, dw) in enumerate(column):
        to_y, to_w = (y + dy) % 2, (w + dw) % 2
        third.append(
            remote(
                q2.at[to_w], p3.at[w, y], y_send.at[n], y_recv.at[n],
                (chan(z, x, to_y, c), to_w),
            )
        )
        third[-1].start()
    p3[w, y] = q2[w]
    for copy in third:
        copy.wait()
    for j in range(4):
        for g in range(2):
            q3[j, g] = p3[g, where[j][2], j]

    a = jnp.where(w == 0, z, x)
    b = jnp.where(w == 0, x, z)
    slots = (pl.ds(0, 2), pl.ds(2, 2))

    def at(s, k, m):
        k, m = (4 - k) % 4, (4 - m) % 4
        return ((a + k) % 4, (b + m) % 4) if s == 0 else ((a + m) % 4, (b + k) % 4)

    def piece(s, k, m, only=None):
        which = slots[s] if only is None else pl.ds(2 * s + only, 1)
        pa, pb = at(s, k, m)
        if m < 2:
            return src_ref.at[which, :, c, pa, pb]
        return late_ref.at[m - 2, which, :, c, pb if s else pa]

    sibling = (chan(z, x, y, 1 - c), w)
    beside = (chan(z, x, 1 - y, c), w)
    keep = pltpu.make_async_copy(q3, src_ref.at[:, :, c, a, b], l_sem.at[1])
    keep.start()
    fourth, fifth, across, last = {}, {}, {}, {}
    for k in (1, 3, 2):
        for s in range(2):
            to = at(s, 4 - k, 0)
            fourth[s, k] = remote(
                q3.at[slots[s]], piece(s, 0, 0), b1_send.at[s, k], b1_recv.at[s, k],
                (plane(w, to[0], to[1], c), w),
            )
            fourth[s, k].start()

    def forward(s, k, m):
        to = at(s, 0, 4 - m)
        only = y if m == 2 else None
        src = piece(s, k, 0, only)
        if k == 0:
            src = q3.at[slots[s] if only is None else pl.ds(2 * s + y, 1)]
        pa, pb = at(s, k, 0)
        dst = piece(s, k, 0)
        if m >= 2:
            which = slots[s] if only is None else pl.ds(2 * s + only, 1)
            dst = late_ref.at[m - 2, which, :, c, pb if s else pa]
        fifth[s, k, m] = remote(
            src, dst, b2_send.at[s, k, m], b2_recv.at[s, k, m], (plane(w, to[0], to[1], c), w)
        )
        fifth[s, k, m].start()

    def share(s, k, m):
        src = q3.at[slots[s]] if k == m == 0 else piece(s, k, m)
        last[s, k, m] = remote(
            src, piece(s, k, m), c_send.at[s, k, m], c_recv.at[s, k, m], sibling
        )
        last[s, k, m].start()

    def products(s, m):
        for k in range(4):
            last[s, k, m].wait()

        def some(n, carry):
            pa, pb = at(s, 0, m)
            pa, pb = (pa, n) if s else (n, pb)
            for e in range(3):
                f = pa * 12 + pb * 3 + e
                left = [src_ref[2 * s + j, :, :, pa, pb, e].reshape(8 * PART, 128) for j in range(2)]
                right = [rhs_ref[g, part, f] for g in range(2) for part in range(2)]
                lines[m, s, n, e] = product(left, right, pairs.at[e])
            return carry

        for n in range(4):
            some(n, 0)
        out = pltpu.make_async_copy(lines.at[m, s], done_ref.at[m, s], o_sem.at[m, s])
        out.start()
        outs.append(out)

    outs = []
    for m in (2, 1, 3):
        for s in range(2):
            forward(s, 0, m)
    for s in range(2):
        share(s, 0, 0)
    keep.wait()
    for k in (1, 3, 2):
        for s in range(2):
            fourth[s, k].wait()
            for m in (2, 1, 3):
                forward(s, k, m)
            share(s, k, 0)
    for copy in windows:
        copy.wait()
    own_rhs.wait()
    hand = pltpu.make_async_copy(rhs_ref, rhs_out, l_sem.at[0])
    hand.start()
    for s in range(2):
        products(s, 0)
    order = (0, 1, 3, 2)
    for k in order:
        for s in range(2):
            fifth[s, k, 2].wait()
            across[s, k] = remote(
                piece(s, k, 2, y), piece(s, k, 2, y), h_send.at[s, k], h_recv.at[s, k], beside
            )
            across[s, k].start()
    for m in (1, 3):
        for k in order:
            for s in range(2):
                fifth[s, k, m].wait()
                share(s, k, m)
    for s in range(2):
        products(s, 1)
    for k in order:
        for s in range(2):
            across[s, k].wait()
            share(s, k, 2)
    for m in (2, 3):
        for k in range(4):
            for s in range(2):
                last[s, k, m].wait()
    for copy in outs:
        copy.wait()
    hand.wait()
    for copy in first:
        copy.wait_send()
    for h in range(2):
        remote(
            v.at[0, pl.ds(0, 12)], p1[h].at[0, 0], a1_send.at[1 - c, h, 0], a1_recv.at[h, 0, 1],
            sibling,
        ).wait_send()


def exchange(block_ids, series):
    dma = pltpu.SemaphoreType.DMA
    vmem = lambda *shape: pltpu.VMEM(shape + (2 * PART, 128), jnp.bfloat16)
    return pl.pallas_call(
        exchange_kernel,
        out_shape=[
            jax.ShapeDtypeStruct((2, 2, 4, 3, 512, 128), jnp.bfloat16),
            jax.ShapeDtypeStruct((2, 4, 2, 2, 4, 3, 2 * PART, 128), jnp.bfloat16),
            jax.ShapeDtypeStruct((2, 2, HALF, 2 * PART, 128), jnp.bfloat16),
        ],
        in_specs=[
            pl.BlockSpec(memory_space=pltpu.SMEM),
            pl.BlockSpec(memory_space=pltpu.VMEM),
            pl.BlockSpec(memory_space=pl.ANY),
        ],
        out_specs=[pl.BlockSpec(memory_space=pl.ANY)] * 3,
        scratch_shapes=[
            pltpu.VMEM((WINS, LENGTH, 128), jnp.bfloat16),
            pltpu.VMEM((2 * NFREQ * PART, 128), jnp.float32),
            vmem(2, NFREQ), vmem(2, 2, HALF), vmem(4, 2, 2, 4, 4, 3),
            pltpu.VMEM((2, 2, 4, 3, 512, 128), jnp.bfloat16),
            pltpu.VMEM((3, 512, 128), jnp.float32),
            vmem(4, 2, 12), vmem(4, 2, 12), vmem(2, 4, 12), vmem(4, 4, 3), vmem(4, 4, 3),
            vmem(2, 4, 3),
            vmem(2, 2, 4, 3), vmem(4, 2, 3),
            dma((WINS // GROUP,)), dma((2, 2)), dma((2,)), dma((2,)), dma((2,)),
            dma((2, 2, 4)), dma((2, 4, 2)), dma((2, 4)), dma((2, 4)), dma((3,)), dma((3,)),
            dma((2, 4)), dma((2, 4)), dma((2, 4, 4)), dma((2, 4, 4)), dma((2, 4)), dma((2, 4)),
            dma((2, 4, 4)), dma((2, 4, 4)),
        ],
        compiler_params=pltpu.CompilerParams(
            collective_id=0, has_side_effects=True, vmem_limit_bytes=42 * 2**20
        ),
    )(block_ids, make_table(), series)


def stack_kernel(done_ref, late_ref, rhs_ref, out_ref, ready, pairs, d_sem, o_sem):
    me = lax.axis_index("chan")
    w = lax.axis_index("win")
    z, x = me // 16, me // 4 % 4
    a = jnp.where(w == 0, z, x)
    b = jnp.where(w == 0, x, z)

    def line(s, m):
        if s == 0:
            return out_ref.at[:, (b - m + 4) % 4, :, 0]
        return out_ref.at[(a - m + 4) % 4, :, :, 1]

    copies = []
    for m in range(2):
        for s in range(2):
            copies.append(
                pltpu.make_async_copy(done_ref.at[m, s], line(s, m), d_sem.at[m, s])
            )
            copies[-1].start()
    for m in (3, 2):
        for s in range(2):
            for n in range(4):
                pa, pb = (a - m + 4) % 4, (b - m + 4) % 4
                pa, pb = (pa, n) if s else (n, pb)
                for e in range(3):
                    f = pa * 12 + pb * 3 + e
                    left = [
                        late_ref[m - 2, 2 * s + j, :, :, n, e].reshape(8 * PART, 128)
                        for j in range(2)
                    ]
                    right = [rhs_ref[g, part, f] for g in range(2) for part in range(2)]
                    ready[m - 2, s, n, e] = product(left, right, pairs.at[n % 2 * 3 + e])
                copies.append(
                    pltpu.make_async_copy(
                        ready.at[m - 2, s, n], out_ref.at[pa, pb, :, s], o_sem.at[m - 2, s, n]
                    )
                )
                copies[-1].start()
    for copy in copies:
        copy.wait()


def stack(done, late, rhs):
    dma = pltpu.SemaphoreType.DMA
    out = pl.pallas_call(
        stack_kernel,
        in_specs=[
            pl.BlockSpec(memory_space=pl.ANY),
            pl.BlockSpec(memory_space=pltpu.VMEM),
            pl.BlockSpec(memory_space=pltpu.VMEM),
        ],
        out_specs=pl.BlockSpec(memory_space=pl.ANY),
        out_shape=jax.ShapeDtypeStruct((4, 4, 3, 2, 512, 128), jnp.bfloat16),
        scratch_shapes=[
            pltpu.VMEM((2, 2, 4, 3, 512, 128), jnp.bfloat16),
            pltpu.VMEM((6, 512, 128), jnp.float32),
            dma((2, 2)),
            dma((2, 2, 4)),
        ],
        compiler_params=pltpu.CompilerParams(vmem_limit_bytes=32 * 2**20),
    )(done, late, rhs)
    return out.reshape(HALF, 512, 2, 128)


def local(series, block_ids):
    return stack(*exchange(block_ids, series))


def solution(mesh):
    return jax.shard_map(
        local,
        mesh=mesh,
        in_specs=(P("win", None, "chan"), P()),
        out_specs=P("win", None, None, "chan"),
        check_vma=False,
    )
```

```python
import functools
import math

import jax
import jax.numpy as jnp
import numpy as np
from jax import lax
from jax.experimental import pallas as pl
from jax.experimental.pallas import tpu as pltpu
from jax.sharding import PartitionSpec as P

LENGTH = 3000
F_LO = 6
NFREQ = 96
WINDOWS = 32
HALF = NFREQ // 2
WINS = WINDOWS // 2
PART = WINS // 2
GROUP = 4
MESH = pl.DeviceIdType.MESH
COL = (((0,), (0,)), ((), ()))


def make_table():
    positions = np.arange(LENGTH)
    bins = F_LO + np.arange(NFREQ)
    angles = 2.0 * math.pi / LENGTH * (bins[:, None] * positions[None, :] % LENGTH)
    hann = 0.5 - 0.5 * np.cos(2.0 * math.pi / LENGTH * positions)
    rows = np.stack([np.cos(angles), -np.sin(angles)], axis=1).reshape(2 * NFREQ, LENGTH)
    return jnp.asarray(rows * hann[None, :], jnp.bfloat16)


def product(left, right, pair):
    tiles = [tile.astype(jnp.float32) * (1.0 / WINDOWS) for tile in right]
    turned = [t for tile in tiles for t in (tile[PART:], -tile[:PART])]
    factor = jnp.concatenate(
        [jnp.concatenate(tiles, axis=0), jnp.concatenate(turned, axis=0)], axis=1
    ).astype(jnp.bfloat16)
    total = lax.dot_general(
        jnp.concatenate(left, axis=1), factor, COL, preferred_element_type=jnp.float32
    )
    pair[pl.ds(0, 256, 2), :] = total[:, :128]
    pair[pl.ds(1, 256, 2), :] = total[:, 128:]
    return pair[...].astype(jnp.bfloat16)


def exchange_kernel(
    ids_ref, table_ref, series_ref, done_ref, late_ref, rhs_out,
    held, rows, v, rhs_ref, src_ref, lines, pairs, p1_0, p1_1, q1, p2_0, p2_1, q2, p3, q3,
    s_sem, o_sem, l_sem, w_send, w_recv, a1_send, a1_recv, a2_send, a2_recv, y_send, y_recv,
    b1_send, b1_recv, b2_send, b2_recv, h_send, h_recv, c_send, c_recv,
):
    me = lax.axis_index("chan")
    w = lax.axis_index("win")
    z, x, y, c = me // 16, me // 4 % 4, me // 2 % 2, me % 2

    def chan(z, x, y, c):
        return ((z * 4 + x) * 2 + y) * 2 + c

    def plane(h, a, b, c):
        return chan(jnp.where(h == 0, a, b), jnp.where(h == 0, b, a), y, c)

    p1 = (p1_0, p1_1)
    p2 = (p2_0, p2_1)
    column = [(0, 1), (1, 0), (1, 1)]
    coords = (z, x)
    loads = []
    for n in range(WINS // GROUP):
        window = pl.ds(n * GROUP, GROUP)
        loads.append(pltpu.make_async_copy(series_ref.at[window], held.at[window], s_sem.at[n]))
        loads[-1].start()

    barrier = pltpu.get_barrier_semaphore()
    peers = [(plane(h, (coords[h] + k) % 4, coords[1 - h], (c + m) % 2), w)
             for h in range(2) for k in range(1, 4) for m in range(2)]
    peers += [(chan(z, x, y, 1 - c), w)]
    peers += [(chan(z, x, (y + dy) % 2, c), (w + dw) % 2) for dy, dw in column]
    for peer in peers:
        pl.semaphore_signal(barrier, inc=1, device_id=peer, device_id_type=MESH)

    def remote(src, dst, send, recv, peer):
        return pltpu.make_async_remote_copy(
            src_ref=src, dst_ref=dst, send_sem=send, recv_sem=recv,
            device_id=peer, device_id_type=MESH,
        )

    def transform(part, n):
        first = part * PART + n * GROUP
        clipped = []
        for k in range(GROUP):
            values = held[first + k].astype(jnp.float32)
            level = 2.0 * jnp.sqrt(jnp.mean(values * values, axis=0, keepdims=True) + 1e-6)
            level = level.astype(jnp.bfloat16)
            clipped.append(jnp.minimum(jnp.maximum(held[first + k], -level), level))
        spectrum = jnp.dot(
            table_ref[...], jnp.concatenate(clipped, axis=1), preferred_element_type=jnp.float32
        )
        power = jnp.sum(spectrum * spectrum, axis=0, keepdims=True) / NFREQ
        whitened = spectrum * lax.rsqrt(power + 1e-6)
        for k in range(GROUP):
            rows[pl.ds(n * GROUP + k, 2 * NFREQ, PART), :] = whitened[:, 128 * k : 128 * (k + 1)]

    first = []
    windows = []
    for part in range(2):
        for n in range(PART // GROUP):
            loads[part * (PART // GROUP) + n].wait()
            transform(part, n)
        v[part] = rows[...].reshape(NFREQ, 2 * PART, 128).astype(jnp.bfloat16)
        if part == 0:
            pl.semaphore_wait(barrier, len(peers))
        other = (c + part) % 2
        for k in (2, 1, 3, 0):
            for h in range(2):
                a, b = coords[h], coords[1 - h]
                to_a = (a + k) % 4
                copy = remote(
                    v.at[part, pl.ds(h * HALF + to_a * 12, 12)], p1[h].at[a, c],
                    a1_send.at[part, h, k], a1_recv.at[h, k, other],
                    (plane(h, to_a, b, part if k else 1 - c), w),
                )
                if k:
                    copy.start()
                    first.append(copy)
                else:
                    pl.when(other == 1)(copy.start)
        windows.append(
            remote(
                v.at[part, pl.ds((1 - w) * HALF, HALF)], rhs_ref.at[w, part],
                w_send.at[part], w_recv.at[part], (me, 1 - w),
            )
        )
        windows[-1].start()
    own_rhs = pltpu.make_async_copy(v.at[:, pl.ds(w * HALF, HALF)], rhs_ref.at[w], l_sem.at[0])
    own_rhs.start()

    where = []
    for j in range(4):
        block = ids_ref[j]
        where.append((block // 16, block // 4 % 4, block // 2 % 2, block % 2))

    second = []
    for h in range(2):
        a, b = coords[h], coords[1 - h]
        p1[h][a, c] = v[c, pl.ds(h * HALF + a * 12, 12)]
        for k in range(4):
            for m in range(2):
                if k or m:
                    remote(
                        v.at[0, pl.ds(0, 12)], p1[h].at[a, c],
                        a1_send.at[0, h, k], a1_recv.at[h, k, m], (me, 1 - w),
                    ).wait_recv()
        for j in range(4):
            q1[h, j] = p1[h][where[j][h], where[j][3]]
        for k in (2, 1, 3):
            to_b = (b + k) % 4
            copy = remote(
                q1.at[h, :, pl.ds(to_b * 3, 3)], p2[h].at[b],
                a2_send.at[h, k], a2_recv.at[h, k], (plane(h, a, to_b, c), w),
            )
            copy.start()
            second.append(copy)
        p2[h][b] = q1[h, :, pl.ds(b * 3, 3)]

    for h in range(2):
        for copy in second[3 * h : 3 * h + 3]:
            copy.wait()
        for j in range(4):
            q2[h, j] = p2[h][where[j][1 - h], j]
    third = []
    for n, (dy, dw) in enumerate(column):
        to_y, to_w = (y + dy) % 2, (w + dw) % 2
        third.append(
            remote(
                q2.at[to_w], p3.at[w, y], y_send.at[n], y_recv.at[n],
                (chan(z, x, to_y, c), to_w),
            )
        )
        third[-1].start()
    p3[w, y] = q2[w]
    for copy in third:
        copy.wait()
    for j in range(4):
        for g in range(2):
            q3[j, g] = p3[g, where[j][2], j]

    a = jnp.where(w == 0, z, x)
    b = jnp.where(w == 0, x, z)
    slots = (pl.ds(0, 2), pl.ds(2, 2))

    def at(s, k, m):
        k, m = (4 - k) % 4, (4 - m) % 4
        return ((a + k) % 4, (b + m) % 4) if s == 0 else ((a + m) % 4, (b + k) % 4)

    def piece(s, k, m, only=None):
        which = slots[s] if only is None else pl.ds(2 * s + only, 1)
        pa, pb = at(s, k, m)
        if m < 2:
            return src_ref.at[which, :, c, pa, pb]
        return late_ref.at[m - 2, which, :, c, pb if s else pa]

    sibling = (chan(z, x, y, 1 - c), w)
    beside = (chan(z, x, 1 - y, c), w)
    keep = pltpu.make_async_copy(q3, src_ref.at[:, :, c, a, b], l_sem.at[1])
    keep.start()
    fourth, fifth, across, last = {}, {}, {}, {}
    for k in (2, 1, 3):
        for s in range(2):
            to = at(s, 4 - k, 0)
            fourth[s, k] = remote(
                q3.at[slots[s]], piece(s, 0, 0), b1_send.at[s, k], b1_recv.at[s, k],
                (plane(w, to[0], to[1], c), w),
            )
            fourth[s, k].start()

    def forward(s, k, m):
        to = at(s, 0, 4 - m)
        only = y if m == 2 else None
        src = piece(s, k, 0, only)
        if k == 0:
            src = q3.at[slots[s] if only is None else pl.ds(2 * s + y, 1)]
        pa, pb = at(s, k, 0)
        dst = piece(s, k, 0)
        if m >= 2:
            which = slots[s] if only is None else pl.ds(2 * s + only, 1)
            dst = late_ref.at[m - 2, which, :, c, pb if s else pa]
        fifth[s, k, m] = remote(
            src, dst, b2_send.at[s, k, m], b2_recv.at[s, k, m], (plane(w, to[0], to[1], c), w)
        )
        fifth[s, k, m].start()

    def share(s, k, m):
        src = q3.at[slots[s]] if k == m == 0 else piece(s, k, m)
        last[s, k, m] = remote(
            src, piece(s, k, m), c_send.at[s, k, m], c_recv.at[s, k, m], sibling
        )
        last[s, k, m].start()

    def products(s, m):
        for k in range(4):
            last[s, k, m].wait()

        def some(n, carry):
            pa, pb = at(s, 0, m)
            pa, pb = (pa, n) if s else (n, pb)
            for e in range(3):
                f = pa * 12 + pb * 3 + e
                left = [src_ref[2 * s + j, :, :, pa, pb, e].reshape(8 * PART, 128) for j in range(2)]
                right = [rhs_ref[g, part, f] for g in range(2) for part in range(2)]
                lines[m, s, n, e] = product(left, right, pairs.at[e])
            return carry

        for n in range(4):
            some(n, 0)
        out = pltpu.make_async_copy(lines.at[m, s], done_ref.at[m, s], o_sem.at[m, s])
        out.start()
        outs.append(out)

    outs = []
    for m in (2, 1, 3):
        for s in range(2):
            forward(s, 0, m)
    for s in range(2):
        share(s, 0, 0)
    keep.wait()
    for k in (1, 3, 2):
        for s in range(2):
            fourth[s, k].wait()
            for m in (2, 1, 3):
                forward(s, k, m)
            share(s, k, 0)
    for copy in windows:
        copy.wait()
    own_rhs.wait()
    hand = pltpu.make_async_copy(rhs_ref, rhs_out, l_sem.at[0])
    hand.start()
    for s in range(2):
        products(s, 0)
    order = (0, 1, 3, 2)
    for k in order:
        for s in range(2):
            fifth[s, k, 2].wait()
            across[s, k] = remote(
                piece(s, k, 2, y), piece(s, k, 2, y), h_send.at[s, k], h_recv.at[s, k], beside
            )
            across[s, k].start()
    for m in (1, 3):
        for k in order:
            for s in range(2):
                fifth[s, k, m].wait()
                share(s, k, m)
    for s in range(2):
        products(s, 1)
    for k in order:
        for s in range(2):
            across[s, k].wait()
            share(s, k, 2)
    for m in (2, 3):
        for k in range(4):
            for s in range(2):
                last[s, k, m].wait()
    for copy in outs:
        copy.wait()
    hand.wait()
    for copy in first:
        copy.wait_send()
    for h in range(2):
        remote(
            v.at[0, pl.ds(0, 12)], p1[h].at[0, 0], a1_send.at[1 - c, h, 0], a1_recv.at[h, 0, 1],
            sibling,
        ).wait_send()


def exchange(block_ids, series):
    dma = pltpu.SemaphoreType.DMA
    vmem = lambda *shape: pltpu.VMEM(shape + (2 * PART, 128), jnp.bfloat16)
    return pl.pallas_call(
        exchange_kernel,
        out_shape=[
            jax.ShapeDtypeStruct((2, 2, 4, 3, 512, 128), jnp.bfloat16),
            jax.ShapeDtypeStruct((2, 4, 2, 2, 4, 3, 2 * PART, 128), jnp.bfloat16),
            jax.ShapeDtypeStruct((2, 2, HALF, 2 * PART, 128), jnp.bfloat16),
        ],
        in_specs=[
            pl.BlockSpec(memory_space=pltpu.SMEM),
            pl.BlockSpec(memory_space=pltpu.VMEM),
            pl.BlockSpec(memory_space=pl.ANY),
        ],
        out_specs=[pl.BlockSpec(memory_space=pl.ANY)] * 3,
        scratch_shapes=[
            pltpu.VMEM((WINS, LENGTH, 128), jnp.bfloat16),
            pltpu.VMEM((2 * NFREQ * PART, 128), jnp.float32),
            vmem(2, NFREQ), vmem(2, 2, HALF), vmem(4, 2, 2, 4, 4, 3),
            pltpu.VMEM((2, 2, 4, 3, 512, 128), jnp.bfloat16),
            pltpu.VMEM((3, 512, 128), jnp.float32),
            vmem(4, 2, 12), vmem(4, 2, 12), vmem(2, 4, 12), vmem(4, 4, 3), vmem(4, 4, 3),
            vmem(2, 4, 3),
            vmem(2, 2, 4, 3), vmem(4, 2, 3),
            dma((WINS // GROUP,)), dma((2, 2)), dma((2,)), dma((2,)), dma((2,)),
            dma((2, 2, 4)), dma((2, 4, 2)), dma((2, 4)), dma((2, 4)), dma((3,)), dma((3,)),
            dma((2, 4)), dma((2, 4)), dma((2, 4, 4)), dma((2, 4, 4)), dma((2, 4)), dma((2, 4)),
            dma((2, 4, 4)), dma((2, 4, 4)),
        ],
        compiler_params=pltpu.CompilerParams(
            collective_id=0, has_side_effects=True, vmem_limit_bytes=42 * 2**20
        ),
    )(block_ids, make_table(), series)


def stack_kernel(done_ref, late_ref, rhs_ref, out_ref, ready, pairs, d_sem, o_sem):
    me = lax.axis_index("chan")
    w = lax.axis_index("win")
    z, x = me // 16, me // 4 % 4
    a = jnp.where(w == 0, z, x)
    b = jnp.where(w == 0, x, z)

    def line(s, m):
        if s == 0:
            return out_ref.at[:, (b - m + 4) % 4, :, 0]
        return out_ref.at[(a - m + 4) % 4, :, :, 1]

    copies = []
    for m in range(2):
        for s in range(2):
            copies.append(
                pltpu.make_async_copy(done_ref.at[m, s], line(s, m), d_sem.at[m, s])
            )
            copies[-1].start()
    for m in (3, 2):
        for s in range(2):
            for n in range(4):
                pa, pb = (a - m + 4) % 4, (b - m + 4) % 4
                pa, pb = (pa, n) if s else (n, pb)
                for e in range(3):
                    f = pa * 12 + pb * 3 + e
                    left = [
                        late_ref[m - 2, 2 * s + j, :, :, n, e].reshape(8 * PART, 128)
                        for j in range(2)
                    ]
                    right = [rhs_ref[g, part, f] for g in range(2) for part in range(2)]
                    ready[m - 2, s, n, e] = product(left, right, pairs.at[n % 2 * 3 + e])
                copies.append(
                    pltpu.make_async_copy(
                        ready.at[m - 2, s, n], out_ref.at[pa, pb, :, s], o_sem.at[m - 2, s, n]
                    )
                )
                copies[-1].start()
    for copy in copies:
        copy.wait()


def stack(done, late, rhs):
    dma = pltpu.SemaphoreType.DMA
    out = pl.pallas_call(
        stack_kernel,
        in_specs=[
            pl.BlockSpec(memory_space=pl.ANY),
            pl.BlockSpec(memory_space=pltpu.VMEM),
            pl.BlockSpec(memory_space=pltpu.VMEM),
        ],
        out_specs=pl.BlockSpec(memory_space=pl.ANY),
        out_shape=jax.ShapeDtypeStruct((4, 4, 3, 2, 512, 128), jnp.bfloat16),
        scratch_shapes=[
            pltpu.VMEM((2, 2, 4, 3, 512, 128), jnp.bfloat16),
            pltpu.VMEM((6, 512, 128), jnp.float32),
            dma((2, 2)),
            dma((2, 2, 4)),
        ],
        compiler_params=pltpu.CompilerParams(vmem_limit_bytes=32 * 2**20),
    )(done, late, rhs)
    return out.reshape(HALF, 512, 2, 128)


def local(series, block_ids):
    return stack(*exchange(block_ids, series))


def solution(mesh):
    return jax.shard_map(
        local,
        mesh=mesh,
        in_specs=(P("win", None, "chan"), P()),
        out_specs=P("win", None, None, "chan"),
        check_vma=False,
    )
```

```python
import functools
import math

import jax
import jax.numpy as jnp
import numpy as np
from jax import lax
from jax.experimental import pallas as pl
from jax.experimental.pallas import tpu as pltpu
from jax.sharding import PartitionSpec as P

LENGTH = 3000
F_LO = 6
NFREQ = 96
WINDOWS = 32
HALF = NFREQ // 2
WINS = WINDOWS // 2
PART = WINS // 2
GROUP = 4
MESH = pl.DeviceIdType.MESH
COL = (((0,), (0,)), ((), ()))


def make_table():
    positions = np.arange(LENGTH)
    bins = F_LO + np.arange(NFREQ)
    angles = 2.0 * math.pi / LENGTH * (bins[:, None] * positions[None, :] % LENGTH)
    hann = 0.5 - 0.5 * np.cos(2.0 * math.pi / LENGTH * positions)
    rows = np.stack([np.cos(angles), -np.sin(angles)], axis=1).reshape(2 * NFREQ, LENGTH)
    return jnp.asarray(rows * hann[None, :], jnp.bfloat16)


def product(left, right, pair):
    tiles = [tile.astype(jnp.float32) * (1.0 / WINDOWS) for tile in right]
    turned = [t for tile in tiles for t in (tile[PART:], -tile[:PART])]
    factor = jnp.concatenate(
        [jnp.concatenate(tiles, axis=0), jnp.concatenate(turned, axis=0)], axis=1
    ).astype(jnp.bfloat16)
    total = lax.dot_general(
        jnp.concatenate(left, axis=1), factor, COL, preferred_element_type=jnp.float32
    )
    pair[pl.ds(0, 256, 2), :] = total[:, :128]
    pair[pl.ds(1, 256, 2), :] = total[:, 128:]
    return pair[...].astype(jnp.bfloat16)


def exchange_kernel(
    ids_ref, table_ref, series_ref, done_ref, late_ref, rhs_out,
    held, rows, v, rhs_ref, src_ref, lines, pairs, p1_0, p1_1, q1, p2_0, p2_1, q2, p3, q3,
    s_sem, o_sem, l_sem, w_send, w_recv, a1_send, a1_recv, a2_send, a2_recv, y_send, y_recv,
    b1_send, b1_recv, b2_send, b2_recv, h_send, h_recv, c_send, c_recv,
):
    me = lax.axis_index("chan")
    w = lax.axis_index("win")
    z, x, y, c = me // 16, me // 4 % 4, me // 2 % 2, me % 2

    def chan(z, x, y, c):
        return ((z * 4 + x) * 2 + y) * 2 + c

    def plane(h, a, b, c):
        return chan(jnp.where(h == 0, a, b), jnp.where(h == 0, b, a), y, c)

    p1 = (p1_0, p1_1)
    p2 = (p2_0, p2_1)
    column = [(0, 1), (1, 0), (1, 1)]
    coords = (z, x)
    loads = []
    for n in range(WINS // GROUP):
        window = pl.ds(n * GROUP, GROUP)
        loads.append(pltpu.make_async_copy(series_ref.at[window], held.at[window], s_sem.at[n]))
        loads[-1].start()

    barrier = pltpu.get_barrier_semaphore()
    peers = [(plane(h, (coords[h] + k) % 4, coords[1 - h], (c + m) % 2), w)
             for h in range(2) for k in range(1, 4) for m in range(2)]
    peers += [(chan(z, x, y, 1 - c), w)]
    peers += [(chan(z, x, (y + dy) % 2, c), (w + dw) % 2) for dy, dw in column]
    for peer in peers:
        pl.semaphore_signal(barrier, inc=1, device_id=peer, device_id_type=MESH)

    def remote(src, dst, send, recv, peer):
        return pltpu.make_async_remote_copy(
            src_ref=src, dst_ref=dst, send_sem=send, recv_sem=recv,
            device_id=peer, device_id_type=MESH,
        )

    def transform(part, n):
        first = part * PART + n * GROUP
        clipped = []
        for k in range(GROUP):
            values = held[first + k].astype(jnp.float32)
            level = 2.0 * jnp.sqrt(jnp.mean(values * values, axis=0, keepdims=True) + 1e-6)
            level = level.astype(jnp.bfloat16)
            clipped.append(jnp.minimum(jnp.maximum(held[first + k], -level), level))
        spectrum = jnp.dot(
            table_ref[...], jnp.concatenate(clipped, axis=1), preferred_element_type=jnp.float32
        )
        power = jnp.sum(spectrum * spectrum, axis=0, keepdims=True) / NFREQ
        whitened = spectrum * lax.rsqrt(power + 1e-6)
        for k in range(GROUP):
            rows[pl.ds(n * GROUP + k, 2 * NFREQ, PART), :] = whitened[:, 128 * k : 128 * (k + 1)]

    first = []
    windows = []
    for part in range(2):
        for n in range(PART // GROUP):
            loads[part * (PART // GROUP) + n].wait()
            transform(part, n)
        v[part] = rows[...].reshape(NFREQ, 2 * PART, 128).astype(jnp.bfloat16)
        if part == 0:
            pl.semaphore_wait(barrier, len(peers))
        other = (c + part) % 2
        for k in (2, 1, 3, 0):
            for h in range(2):
                a, b = coords[h], coords[1 - h]
                to_a = (a + k) % 4
                copy = remote(
                    v.at[part, pl.ds(h * HALF + to_a * 12, 12)], p1[h].at[a, c],
                    a1_send.at[part, h, k], a1_recv.at[h, k, other],
                    (plane(h, to_a, b, part if k else 1 - c), w),
                )
                if k:
                    copy.start()
                    first.append(copy)
                else:
                    pl.when(other == 1)(copy.start)
        windows.append(
            remote(
                v.at[part, pl.ds((1 - w) * HALF, HALF)], rhs_ref.at[w, part],
                w_send.at[part], w_recv.at[part], (me, 1 - w),
            )
        )
        windows[-1].start()
    own_rhs = pltpu.make_async_copy(v.at[:, pl.ds(w * HALF, HALF)], rhs_ref.at[w], l_sem.at[0])
    own_rhs.start()

    where = []
    for j in range(4):
        block = ids_ref[j]
        where.append((block // 16, block // 4 % 4, block // 2 % 2, block % 2))

    second = []
    for h in range(2):
        a, b = coords[h], coords[1 - h]
        p1[h][a, c] = v[c, pl.ds(h * HALF + a * 12, 12)]
        for k in range(4):
            for m in range(2):
                if k or m:
                    remote(
                        v.at[0, pl.ds(0, 12)], p1[h].at[a, c],
                        a1_send.at[0, h, k], a1_recv.at[h, k, m], (me, 1 - w),
                    ).wait_recv()
        for j in range(4):
            q1[h, j] = p1[h][where[j][h], where[j][3]]
        for k in (2, 1, 3):
            to_b = (b + k) % 4
            copy = remote(
                q1.at[h, :, pl.ds(to_b * 3, 3)], p2[h].at[b],
                a2_send.at[h, k], a2_recv.at[h, k], (plane(h, a, to_b, c), w),
            )
            copy.start()
            second.append(copy)
        p2[h][b] = q1[h, :, pl.ds(b * 3, 3)]

    for h in range(2):
        for copy in second[3 * h : 3 * h + 3]:
            copy.wait()
        for j in range(4):
            q2[h, j] = p2[h][where[j][1 - h], j]
    third = []
    for n, (dy, dw) in enumerate(column):
        to_y, to_w = (y + dy) % 2, (w + dw) % 2
        third.append(
            remote(
                q2.at[to_w], p3.at[w, y], y_send.at[n], y_recv.at[n],
                (chan(z, x, to_y, c), to_w),
            )
        )
        third[-1].start()
    p3[w, y] = q2[w]
    for copy in third:
        copy.wait()
    for j in range(4):
        for g in range(2):
            q3[j, g] = p3[g, where[j][2], j]

    a = jnp.where(w == 0, z, x)
    b = jnp.where(w == 0, x, z)
    slots = (pl.ds(0, 2), pl.ds(2, 2))

    def at(s, k, m):
        k, m = (4 - k) % 4, (4 - m) % 4
        return ((a + k) % 4, (b + m) % 4) if s == 0 else ((a + m) % 4, (b + k) % 4)

    def piece(s, k, m, only=None):
        which = slots[s] if only is None else pl.ds(2 * s + only, 1)
        pa, pb = at(s, k, m)
        if m < 2:
            return src_ref.at[which, :, c, pa, pb]
        return late_ref.at[m - 2, which, :, c, pb if s else pa]

    sibling = (chan(z, x, y, 1 - c), w)
    beside = (chan(z, x, 1 - y, c), w)
    keep = pltpu.make_async_copy(q3, src_ref.at[:, :, c, a, b], l_sem.at[1])
    keep.start()
    fourth, fifth, across, last = {}, {}, {}, {}
    for k in (2, 1, 3):
        for s in range(2):
            to = at(s, 4 - k, 0)
            fourth[s, k] = remote(
                q3.at[slots[s]], piece(s, 0, 0), b1_send.at[s, k], b1_recv.at[s, k],
                (plane(w, to[0], to[1], c), w),
            )
            fourth[s, k].start()

    def forward(s, k, m):
        to = at(s, 0, 4 - m)
        only = y if m == 2 else None
        src = piece(s, k, 0, only)
        if k == 0:
            src = q3.at[slots[s] if only is None else pl.ds(2 * s + y, 1)]
        pa, pb = at(s, k, 0)
        dst = piece(s, k, 0)
        if m >= 2:
            which = slots[s] if only is None else pl.ds(2 * s + only, 1)
            dst = late_ref.at[m - 2, which, :, c, pb if s else pa]
        fifth[s, k, m] = remote(
            src, dst, b2_send.at[s, k, m], b2_recv.at[s, k, m], (plane(w, to[0], to[1], c), w)
        )
        fifth[s, k, m].start()

    def share(s, k, m):
        src = q3.at[slots[s]] if k == m == 0 else piece(s, k, m)
        last[s, k, m] = remote(
            src, piece(s, k, m), c_send.at[s, k, m], c_recv.at[s, k, m], sibling
        )
        last[s, k, m].start()

    def products(s, m):
        for k in range(4):
            last[s, k, m].wait()

        def some(n, carry):
            pa, pb = at(s, 0, m)
            pa, pb = (pa, n) if s else (n, pb)
            for e in range(3):
                f = pa * 12 + pb * 3 + e
                left = [src_ref[2 * s + j, :, :, pa, pb, e].reshape(8 * PART, 128) for j in range(2)]
                right = [rhs_ref[g, part, f] for g in range(2) for part in range(2)]
                lines[m, s, n, e] = product(left, right, pairs.at[n % 2 * 3 + e])
            return carry

        for n in range(4):
            some(n, 0)
        out = pltpu.make_async_copy(lines.at[m, s], done_ref.at[m, s], o_sem.at[m, s])
        out.start()
        outs.append(out)

    outs = []
    for m in (2, 1, 3):
        for s in range(2):
            forward(s, 0, m)
    for s in range(2):
        share(s, 0, 0)
    keep.wait()
    for k in (1, 3, 2):
        for s in range(2):
            fourth[s, k].wait()
            for m in (2, 1, 3):
                forward(s, k, m)
            share(s, k, 0)
    for copy in windows:
        copy.wait()
    own_rhs.wait()
    hand = pltpu.make_async_copy(rhs_ref, rhs_out, l_sem.at[0])
    hand.start()
    for s in range(2):
        products(s, 0)
    order = (0, 1, 3, 2)
    for k in order:
        for s in range(2):
            fifth[s, k, 2].wait()
            across[s, k] = remote(
                piece(s, k, 2, y), piece(s, k, 2, y), h_send.at[s, k], h_recv.at[s, k], beside
            )
            across[s, k].start()
    for m in (1, 3):
        for k in order:
            for s in range(2):
                fifth[s, k, m].wait()
                share(s, k, m)
    for s in range(2):
        products(s, 1)
    for k in order:
        for s in range(2):
            across[s, k].wait()
            share(s, k, 2)
    for m in (2, 3):
        for k in range(4):
            for s in range(2):
                last[s, k, m].wait()
    for copy in outs:
        copy.wait()
    hand.wait()
    for copy in first:
        copy.wait_send()
    for h in range(2):
        remote(
            v.at[0, pl.ds(0, 12)], p1[h].at[0, 0], a1_send.at[1 - c, h, 0], a1_recv.at[h, 0, 1],
            sibling,
        ).wait_send()


def exchange(block_ids, series):
    dma = pltpu.SemaphoreType.DMA
    vmem = lambda *shape: pltpu.VMEM(shape + (2 * PART, 128), jnp.bfloat16)
    return pl.pallas_call(
        exchange_kernel,
        out_shape=[
            jax.ShapeDtypeStruct((2, 2, 4, 3, 512, 128), jnp.bfloat16),
            jax.ShapeDtypeStruct((2, 4, 2, 2, 4, 3, 2 * PART, 128), jnp.bfloat16),
            jax.ShapeDtypeStruct((2, 2, HALF, 2 * PART, 128), jnp.bfloat16),
        ],
        in_specs=[
            pl.BlockSpec(memory_space=pltpu.SMEM),
            pl.BlockSpec(memory_space=pltpu.VMEM),
            pl.BlockSpec(memory_space=pl.ANY),
        ],
        out_specs=[pl.BlockSpec(memory_space=pl.ANY)] * 3,
        scratch_shapes=[
            pltpu.VMEM((WINS, LENGTH, 128), jnp.bfloat16),
            pltpu.VMEM((2 * NFREQ * PART, 128), jnp.float32),
            vmem(2, NFREQ), vmem(2, 2, HALF), vmem(4, 2, 2, 4, 4, 3),
            pltpu.VMEM((2, 2, 4, 3, 512, 128), jnp.bfloat16),
            pltpu.VMEM((6, 512, 128), jnp.float32),
            vmem(4, 2, 12), vmem(4, 2, 12), vmem(2, 4, 12), vmem(4, 4, 3), vmem(4, 4, 3),
            vmem(2, 4, 3),
            vmem(2, 2, 4, 3), vmem(4, 2, 3),
            dma((WINS // GROUP,)), dma((2, 2)), dma((2,)), dma((2,)), dma((2,)),
            dma((2, 2, 4)), dma((2, 4, 2)), dma((2, 4)), dma((2, 4)), dma((3,)), dma((3,)),
            dma((2, 4)), dma((2, 4)), dma((2, 4, 4)), dma((2, 4, 4)), dma((2, 4)), dma((2, 4)),
            dma((2, 4, 4)), dma((2, 4, 4)),
        ],
        compiler_params=pltpu.CompilerParams(
            collective_id=0, has_side_effects=True, vmem_limit_bytes=42 * 2**20
        ),
    )(block_ids, make_table(), series)


def stack_kernel(done_ref, late_ref, rhs_ref, out_ref, ready, pairs, d_sem, o_sem):
    me = lax.axis_index("chan")
    w = lax.axis_index("win")
    z, x = me // 16, me // 4 % 4
    a = jnp.where(w == 0, z, x)
    b = jnp.where(w == 0, x, z)

    def line(s, m):
        if s == 0:
            return out_ref.at[:, (b - m + 4) % 4, :, 0]
        return out_ref.at[(a - m + 4) % 4, :, :, 1]

    copies = []
    for m in range(2):
        for s in range(2):
            copies.append(
                pltpu.make_async_copy(done_ref.at[m, s], line(s, m), d_sem.at[m, s])
            )
            copies[-1].start()
    for m in (3, 2):
        for s in range(2):
            for n in range(4):
                pa, pb = (a - m + 4) % 4, (b - m + 4) % 4
                pa, pb = (pa, n) if s else (n, pb)
                for e in range(3):
                    f = pa * 12 + pb * 3 + e
                    left = [
                        late_ref[m - 2, 2 * s + j, :, :, n, e].reshape(8 * PART, 128)
                        for j in range(2)
                    ]
                    right = [rhs_ref[g, part, f] for g in range(2) for part in range(2)]
                    ready[m - 2, s, n, e] = product(left, right, pairs.at[n % 2 * 3 + e])
                copies.append(
                    pltpu.make_async_copy(
                        ready.at[m - 2, s, n], out_ref.at[pa, pb, :, s], o_sem.at[m - 2, s, n]
                    )
                )
                copies[-1].start()
    for copy in copies:
        copy.wait()


def stack(done, late, rhs):
    dma = pltpu.SemaphoreType.DMA
    out = pl.pallas_call(
        stack_kernel,
        in_specs=[
            pl.BlockSpec(memory_space=pl.ANY),
            pl.BlockSpec(memory_space=pltpu.VMEM),
            pl.BlockSpec(memory_space=pltpu.VMEM),
        ],
        out_specs=pl.BlockSpec(memory_space=pl.ANY),
        out_shape=jax.ShapeDtypeStruct((4, 4, 3, 2, 512, 128), jnp.bfloat16),
        scratch_shapes=[
            pltpu.VMEM((2, 2, 4, 3, 512, 128), jnp.bfloat16),
            pltpu.VMEM((6, 512, 128), jnp.float32),
            dma((2, 2)),
            dma((2, 2, 4)),
        ],
        compiler_params=pltpu.CompilerParams(vmem_limit_bytes=32 * 2**20),
    )(done, late, rhs)
    return out.reshape(HALF, 512, 2, 128)


def local(series, block_ids):
    return stack(*exchange(block_ids, series))


def solution(mesh):
    return jax.shard_map(
        local,
        mesh=mesh,
        in_specs=(P("win", None, "chan"), P()),
        out_specs=P("win", None, None, "chan"),
        check_vma=False,
    )
```
